128 devices in a mesh: blk: 32 (over y, x_hi, z), head: 4 (over x_lo, core).
Axes of the slice: x: 4 (x_hi: 2, x_lo: 2; x = x_hi * 2 + x_lo), y: 4, z: 4, core: 2. Of those that a mesh axis runs over, the one named last changes fastest.
Arguments:
- img_qkv: bfloat16 [12288, 9216], P(('blk', 'head')), may hold values from -6 to 6
- txt_qkv: bfloat16 [512, 9216], P(('blk', 'head')), may hold values from -6 to 6
- q_gain: float32 [128], replicated, may hold values from 1.4 to 6.5
- k_gain: float32 [128], replicated, may hold values from 1.4 to 6.5
Outputs:
- img_out: bfloat16 [12288, 3072], P(('blk', 'head'))
- txt_out: bfloat16 [512, 3072], P(('blk', 'head'))
The draws below stay inside these ranges and needn't reach their ends.
All inputs are finite; a program needn't handle non-finite values.
Results may differ from the reference program's by a relative error of at most 0.0065.
The reference program's roundings to bfloat16 on the way count: a program that leaves them out, or rounds other values in their place, can miss the bound.
Values may be sent and summed in bfloat16 or wider, within the bound.
A program may use at most 128 MiB of HBM per device.

```python
import jax
import jax.numpy as jnp
from jax import lax

D = 3072
HEADS = 24
HEAD_DIM = 128
GRID_W = 128
IMG = 12288
TXT = 512
N_BLK = 32


def draw_txt_qkv(key, part):
    key = jax.random.fold_in(key, 11)
    first_key = jax.random.fold_in(key, 0)
    drawn = jnp.clip(jax.random.normal(first_key, (TXT, 3, D), jnp.float32), -6.0, 6.0)
    return drawn.reshape(TXT, 3 * D).astype(jnp.bfloat16)


def draw_q_gain(key, part):
    key = jax.random.fold_in(key, 21)
    drawn = jax.random.uniform(key, (HEAD_DIM,), jnp.float32, 1.4, 2.2)
    return drawn


def draw_k_gain(key, part):
    key = jax.random.fold_in(key, 22)
    drawn = jax.random.uniform(key, (HEAD_DIM,), jnp.float32, 1.4, 2.2)
    return drawn


def levels(key, extent, pieces, low, top_value):
    def one(dim, blocks):
        steps = jax.random.uniform(jax.random.fold_in(jax.random.fold_in(key, 6), dim), (blocks,), jnp.float32, low / len(pieces), top_value / len(pieces))
        return jnp.repeat(jnp.exp(steps), extent[dim] // blocks).reshape((-1,) + (1,) * (len(extent) - dim - 1))

    loudness = one(*pieces[0])
    for cut in pieces[1:]:
        loudness = loudness * one(*cut)
    return loudness


def noise(stream_key, extent, width, reach, cuts=(), kind=jnp.bfloat16):
    result = width * jax.random.normal(stream_key, extent, jnp.float32)
    if cuts:
        result = result * levels(stream_key, extent, cuts, -0.22, 0.18)
    return jnp.clip(result, -reach, reach).astype(kind)


def setup_inputs(seed: int = 0) -> dict:
    streams_of = jax.random.split(jax.random.key(seed), 5)
    return {
        "img_qkv": noise(streams_of[0], (IMG, 3 * D), 1.0, 6.0, ((0, 128),)),
        "txt_qkv": draw_txt_qkv(jax.random.fold_in(streams_of[4], 71), 0),
        "q_gain": draw_q_gain(jax.random.fold_in(streams_of[4], 71), 0),
        "k_gain": draw_k_gain(jax.random.fold_in(streams_of[4], 71), 0),
    }


EPSILON = 1e-06

def split_heads(packed):
    return packed.reshape(packed.shape[0], 3, HEADS, HEAD_DIM)

def normalize(projected, gains):
    projected = projected.astype(jnp.float32)
    return projected * lax.rsqrt(lax.optimization_barrier(jnp.mean(projected * projected, axis=-1, keepdims=True)) + EPSILON) * gains

def axis_freqs(pair_count):
    return 10000.0 ** (-(jnp.arange(pair_count, dtype=jnp.float32) / pair_count))

def rope_angles(token_index, half_img):
    frame_pairs = HEAD_DIM // 16
    side_pairs = (HEAD_DIM // 2 - frame_pairs) // 2
    frame_pos = (token_index // half_img).astype(jnp.float32)
    within = token_index % half_img
    row_pos = (within // GRID_W).astype(jnp.float32)
    col_pos = (within % GRID_W).astype(jnp.float32)
    return jnp.concatenate([frame_pos[:, None] * axis_freqs(frame_pairs)[None, :], row_pos[:, None] * axis_freqs(side_pairs)[None, :], col_pos[:, None] * axis_freqs(side_pairs)[None, :]], axis=1)

def rotate(projected, angles):
    tokens_here, heads_here, dims_here = projected.shape
    pairs = projected.reshape(tokens_here, heads_here, dims_here // 2, 2)
    cosine = jnp.cos(angles)[:, None, :]
    sine = jnp.sin(angles)[:, None, :]
    first = pairs[..., 0]
    second = pairs[..., 1]
    return jnp.stack([cosine * first - sine * second, sine * first + cosine * second], axis=-1).reshape(projected.shape)

def reference(img_qkv, txt_qkv, q_gain, k_gain):
    image_parts = split_heads(img_qkv)
    text_parts = split_heads(txt_qkv)
    angles = rope_angles(jnp.arange(IMG, dtype=jnp.int32), IMG // 2)
    img_query = rotate(normalize(image_parts[:, 0], q_gain), angles).astype(jnp.bfloat16)
    img_key = rotate(normalize(image_parts[:, 1], k_gain), angles).astype(jnp.bfloat16)
    txt_query = normalize(text_parts[:, 0], q_gain).astype(jnp.bfloat16)
    txt_key = normalize(text_parts[:, 1], k_gain).astype(jnp.bfloat16)
    queries = jnp.concatenate([txt_query, img_query], axis=0).transpose(1, 0, 2)
    keys_all = jnp.concatenate([txt_key, img_key], axis=0).transpose(1, 0, 2)
    values_all = jnp.concatenate([text_parts[:, 2], image_parts[:, 2]], axis=0).transpose(1, 0, 2)
    joint_rows = TXT + IMG
    block_rows = joint_rows // N_BLK
    score_scale = HEAD_DIM ** (-0.5)

    def one_head(operands):
        head_query, head_key, head_value = operands

        def one_block(query_block):
            scores = jnp.dot(query_block, head_key.T, preferred_element_type=jnp.float32) * score_scale
            row_top = lax.optimization_barrier(jnp.max(scores, axis=1, keepdims=True))
            weights = jnp.exp(scores - row_top)
            weight_sum = lax.optimization_barrier(jnp.sum(weights, axis=1, keepdims=True))
            attended = jnp.dot(weights.astype(jnp.bfloat16), head_value, preferred_element_type=jnp.float32) / weight_sum
            return attended.astype(jnp.bfloat16)
        return lax.map(one_block, head_query.reshape(N_BLK, block_rows, HEAD_DIM)).reshape(joint_rows, HEAD_DIM)
    attended = lax.map(one_head, (queries, keys_all, values_all))
    attended = attended.transpose(1, 0, 2).reshape(joint_rows, D)
    return (attended[TXT:], attended[:TXT])
```

```python
import functools

import jax
import jax.numpy as jnp
from jax import lax
from jax.experimental import pallas as pl
from jax.experimental.pallas import tpu as pltpu
from jax.sharding import PartitionSpec as P

HEADS = 24
HD = 128
GRID_W = 128
EPSILON = 1e-06
GROUPS = 4
LH = HEADS // GROUPS
MESH = pl.DeviceIdType.MESH
LOG2E = 1.4426950408889634
BF = jnp.bfloat16
F32 = jnp.float32


def axis_freqs(pair_count):
    return 10000.0 ** (-(jnp.arange(pair_count, dtype=jnp.float32) / pair_count))


def dot(a, b, dims):
    return lax.dot_general(a, b, (dims, ((), ())), preferred_element_type=jnp.float32)


def kernel(
    img_ref, txt_ref, gain_ref, freq_ref, out_img, out_txt,
    kv_send, q_send, tx_f32, tx_send, tx_land, kv_all, q_all, s_a, s_b,
    o_send, l_send, o_land, l_land, o_own, l_own, result, txt_land,
    cs_ref, max_ref,
    loc_sem, tl_sem, zkv_s, zkv_r, zq_s, zq_r, zt_s, zt_r,
    xs_s, xs_r, xf_s, xf_r, sb_s, sb_r, yq_s, yq_r, yo_s, yo_r, yl_s, yl_r,
    hi_s, hi_r, ht_s, ht_r, hl_sem,
):
    rows = img_ref.shape[0]
    trows = txt_ref.shape[0]
    blk_rows = GROUPS * (rows + trows)
    img_part = GROUPS * rows
    width = HEADS * HD
    blk = lax.axis_index("blk")
    head = lax.axis_index("head")
    y = blk // 8
    x = ((blk // 4) % 2) * 2 + head // 2
    z = blk % 4
    c = head % 2

    def at(xx, yy, zz, cc):
        return ((yy % 4) * 8 + ((xx % 4) // 2) * 4 + zz % 4, (xx % 2) * 2 + cc)

    def al(v, n):
        return pl.multiple_of(v, n)

    partners = [at(x, y, z + d, c) for d in (1, 2, 3)]
    partners += [at(x, y + d, z, c) for d in (1, 2, 3)]
    partners += [at(x + 1, y, z, c), at(x + 3, y, z, c), at(x, y, z, 1 - c)]
    barrier = pltpu.get_barrier_semaphore()
    for p in partners:
        pl.semaphore_signal(barrier, inc=1, device_id=p, device_id_type=MESH)

    def rc(src, dst, ss, rs, to):
        return pltpu.make_async_remote_copy(
            src_ref=src, dst_ref=dst, send_sem=ss, recv_sem=rs, device_id=to, device_id_type=MESH
        )

    def kv_block(h, which):
        return kv_all.at[h, :, pl.ds(al(which * blk_rows, 16), blk_rows), :]

    def slot(xx, cc):
        return (xx % 4) * 2 + cc

    own = slot(x, c)

    def zkv(h, d, frm):
        return rc(
            kv_send.at[(z + d) % 4, h],
            kv_all.at[h, :, pl.ds(al(own * blk_rows + frm * rows, 16), rows), :],
            zkv_s.at[h, d - 1], zkv_r.at[h, d - 1], at(x, y, z + d, c),
        )

    def zq(h, d, frm):
        return rc(
            q_send.at[(z + d) % 4, h],
            q_all.at[h, y, pl.ds(al(frm * rows, 16), rows), :],
            zq_s.at[h, d - 1], zq_r.at[h, d - 1], at(x, y, z + d, c),
        )

    def zt(d, frm):
        return rc(
            tx_send.at[(z + d) % 4], tx_land.at[frm],
            zt_s.at[d - 1], zt_r.at[d - 1], at(x, y, z + d, c),
        )

    def lkv(h):
        return pltpu.make_async_copy(
            kv_send.at[z, h],
            kv_all.at[h, :, pl.ds(al(own * blk_rows + z * rows, 16), rows), :],
            loc_sem.at[h, 0],
        )

    def lq(h):
        return pltpu.make_async_copy(
            q_send.at[z, h], q_all.at[h, y, pl.ds(al(z * rows, 16), rows), :], loc_sem.at[h, 1]
        )

    def xs(h, i, which):
        b = kv_block(h, which)
        return rc(b, b, xs_s.at[h, i], xs_r.at[h, i], at(x + (1 if i == 0 else 3), y, z, c))

    def xf(h, i, which):
        b = kv_all.at[h, i, pl.ds(al(which * blk_rows, 16), blk_rows), :]
        return rc(b, b, xf_s.at[h, i], xf_r.at[h, i], at(x + (1 if i == 0 else 3), y, z, c))

    def sb(h, i, which):
        b = kv_block(h, which)
        return rc(b, b, sb_s.at[h, i], sb_r.at[h, i], at(x, y, z, 1 - c))

    def yq(h, d, frm):
        b = q_all.at[h, frm]
        return rc(b, b, yq_s.at[h, d - 1], yq_r.at[h, d - 1], at(x, y + d, z, c))

    def yo(h, i):
        return rc(
            o_send.at[h, i], o_land.at[h, i], yo_s.at[h, i], yo_r.at[h, i], at(x, y + i + 1, z, c)
        )

    def yl(h, i):
        return rc(
            l_send.at[h, i], l_land.at[h, i], yl_s.at[h, i], yl_r.at[h, i], at(x, y + i + 1, z, c)
        )

    def hi(h, d, frm):
        return rc(
            result.at[h, pl.ds(al(((z + d) % 4) * rows, 16), rows), :],
            out_img.at[:, pl.ds(al((frm * LH + h) * HD, HD), HD)],
            hi_s.at[h, d - 1], hi_r.at[h, d - 1], at(x, y, z + d, c),
        )

    def ht(h, d, frm):
        return rc(
            result.at[h, pl.ds(img_part, GROUPS * trows), :],
            txt_land.at[:, pl.ds(al((frm * LH + h) * HD, HD), HD)],
            ht_s.at[h, d - 1], ht_r.at[h, d - 1], at(x, y, z + d, c),
        )

    def hl(h, i):
        lanes = pl.ds(al((z * LH + h) * HD, HD), HD)
        if i == 0:
            return pltpu.make_async_copy(
                result.at[h, pl.ds(al(z * rows, 16), rows), :], out_img.at[:, lanes], hl_sem.at[h, 0]
            )
        return pltpu.make_async_copy(
            result.at[h, pl.ds(img_part, GROUPS * trows), :], txt_land.at[:, lanes], hl_sem.at[h, 1]
        )

    device = blk * 4 + head
    half_devices = 64
    lane = lax.broadcasted_iota(jnp.int32, (rows, HD), 1)
    pair = lane // 2
    within = (device % half_devices) * rows + lax.broadcasted_iota(jnp.int32, (rows, HD), 0)
    frame_pairs = HD // 16
    side_pairs = (HD // 2 - frame_pairs) // 2
    frame_pos = jnp.full((rows, HD), device // half_devices, jnp.int32)
    position = jnp.where(
        pair < frame_pairs,
        frame_pos,
        jnp.where(pair < frame_pairs + side_pairs, within // GRID_W, within % GRID_W),
    )
    angles = position.astype(F32) * freq_ref[0:1, :]
    cs_ref[0] = jnp.cos(angles)
    cs_ref[1] = jnp.where(lane % 2 == 0, -1.0, 1.0) * jnp.sin(angles)

    def normal(v, gain):
        return v * lax.rsqrt(jnp.mean(v * v, axis=-1, keepdims=True) + EPSILON) * gain

    def rope(v):
        even = lax.broadcasted_iota(jnp.int32, v.shape, 1) % 2 == 0
        swapped = jnp.where(even, pltpu.roll(v, HD - 1, 1), pltpu.roll(v, 1, 1))
        return cs_ref[0] * v + cs_ref[1] * swapped

    for g in range(GROUPS):
        for part in range(3):
            for h in range(LH):
                lo = part * width + (g * LH + h) * HD
                v = txt_ref[:, lo : lo + HD].astype(F32)
                if part < 2:
                    v = normal(v, gain_ref[part : part + 1, :])
                r = part * LH * trows + h * trows
                tx_f32[g, r : r + trows, :] = v
        used = 3 * LH * trows
        tx_f32[g, used:, :] = jnp.zeros((tx_f32.shape[1] - used, HD), F32)
        tx_send[g] = tx_f32[g].astype(BF)

    pl.semaphore_wait(barrier, len(partners))
    for d in (1, 2, 3):
        zt(d, z).start()
    tl = pltpu.make_async_copy(tx_send.at[z], tx_land.at[z], tl_sem)
    tl.start()

    def prep(h, carry):
        for g in range(GROUPS):
            base = (g * LH + h) * HD
            k = img_ref[:, pl.ds(al(width + base, HD), HD)].astype(F32)
            kv_send[g, h, 0] = rope(normal(k, gain_ref[1:2, :])).astype(BF)
            kv_send[g, h, 1] = img_ref[:, pl.ds(al(2 * width + base, HD), HD)]
            q = img_ref[:, pl.ds(al(base, HD), HD)].astype(F32)
            q_send[g, h] = rope(normal(q, gain_ref[0:1, :])).astype(BF)
        for d in (1, 2, 3):
            zkv(h, d, z).start()
        for d in (1, 2, 3):
            zq(h, d, z).start()
        lkv(h).start()
        lq(h).start()
        return carry

    lax.fori_loop(0, LH, prep, 0)

    for d in (1, 2, 3):
        zt(d, (z - d) % 4).wait_recv()
    tl.wait()
    pad = tx_land.shape[1]
    tr = GROUPS * trows
    row = lax.broadcasted_iota(jnp.int32, (tr, GROUPS * pad), 0)
    col = lax.broadcasted_iota(jnp.int32, (tr, GROUPS * pad), 1)
    target = (row // trows) * pad + row % trows
    pick = jnp.concatenate(
        [
            jnp.where(col == target + j * trows, 1.0, 0.0).astype(BF)
            for j in range(3 * LH)
        ],
        axis=0,
    )
    texts = dot(pick, tx_land[...].reshape(GROUPS * pad, HD), ((1,), (0,))).astype(BF)
    for h in range(LH):
        q_all[h, y, img_part:, :] = texts[h * tr : (h + 1) * tr]
        for part in (0, 1):
            r = ((part + 1) * LH + h) * tr
            kv_all[h, part, pl.ds(al(own * blk_rows + img_part, 16), tr), :] = texts[r : r + tr]

    def stage_a(h):
        for d in (1, 2, 3):
            zkv(h, d, (z - d) % 4).wait_recv()
        lkv(h).wait()
        xs(h, 0, own).start()
        xs(h, 1, own).start()
        sb(h, 0, own).start()
        for d in (1, 2, 3):
            zq(h, d, (z - d) % 4).wait_recv()
        lq(h).wait()
        for d in (1, 2, 3):
            yq(h, d, y).start()

    def stage_b(h):
        left, right = slot(x + 3, c), slot(x + 1, c)
        xs(h, 0, left).wait_recv()
        xf(h, 0, left).start()
        xs(h, 1, right).wait_recv()
        xf(h, 1, right).start()
        sb(h, 1, left).start()
        sb(h, 2, right).start()

    def stage_c(h):
        far = slot(x + 2, c)
        xf(h, 0, far).wait_recv()
        xf(h, 1, far).wait_recv()
        sb(h, 3, far).start()

    def stage_d(h):
        for i, dx in enumerate((0, 3, 1, 2)):
            sb(h, i, slot(x + dx, 1 - c)).wait_recv()
        for d in (1, 2, 3):
            yq(h, d, (y - d) % 4).wait_recv()

    scale = LOG2E * HD**-0.5
    n_keys = kv_all.shape[2]

    def fill(h, i, s_ref):
        q = q_all[h, (y + i + 1) % 4].astype(F32) * scale
        high = q.astype(BF)
        low = (q - high.astype(F32)).astype(BF)
        k = kv_all[h, 0]
        s = dot(
            jnp.concatenate([high, low], axis=1), jnp.concatenate([k, k], axis=1), ((1,), (1,))
        )
        s_ref[...] = s
        top = s[:, 0:HD]
        for t in range(1, n_keys // HD):
            top = jnp.maximum(top, s[:, t * HD : (t + 1) * HD])
        return top

    eye = lax.broadcasted_iota(jnp.int32, (HD, HD), 0) == lax.broadcasted_iota(
        jnp.int32, (HD, HD), 1
    )

    def rows_to_lanes(v):
        lines = []
        for r in range(0, blk_rows, HD):
            n = min(HD, blk_rows - r)
            lines.append(jnp.sum(jnp.where(eye[:n], v[r : r + n], 0.0), axis=0, keepdims=True))
        lines.append(jnp.zeros((8 - len(lines), HD), F32))
        return jnp.concatenate(lines, axis=0)

    def lanes_to_rows(v):
        parts = []
        for j, r in enumerate(range(0, blk_rows, HD)):
            n = min(HD, blk_rows - r)
            line = jnp.broadcast_to(v[j : j + 1], (n, HD))
            parts.append(jnp.sum(jnp.where(eye[:n], line, 0.0), axis=1, keepdims=True))
        return jnp.concatenate(parts, axis=0)

    def step(h, i, s_in, s_out, h_next, i_next):
        m = jnp.max(max_ref[...], axis=1, keepdims=True)
        top = fill(h_next, i_next, s_out)
        p = jnp.exp2(s_in[...] - m).astype(BF)
        v = kv_all[h, 1]
        acc = dot(p, jnp.concatenate([v, jnp.ones_like(v)], axis=1), ((1,), (0,)))
        max_ref[...] = top
        total = acc[:, HD:]
        o = (acc[:, :HD] / total).astype(BF)
        lse = m + jnp.log2(total)
        if i < 3:
            o_send[h, i] = o
            l_send[h, i] = rows_to_lanes(lse)
            yo(h, i).start()
            yl(h, i).start()
        else:
            o_own[...] = o
            l_own[...] = lse

    def combine(h):
        for i in range(3):
            yo(h, i).wait_recv()
            yl(h, i).wait_recv()
        ls = [l_own[...]] + [lanes_to_rows(l_land[h, i]) for i in range(3)]
        top = functools.reduce(jnp.maximum, ls)
        ws = [jnp.exp2(v - top) for v in ls]
        norm = 1.0 / (ws[0] + ws[1] + ws[2] + ws[3])
        o = o_own[...].astype(F32) * ws[0]
        for i in range(3):
            o = o + o_land[h, i].astype(F32) * ws[i + 1]
        result[h] = (o * norm).astype(BF)
        for d in (1, 2, 3):
            hi(h, d, z).start()
            ht(h, d, z).start()
        hl(h, 0).start()
        hl(h, 1).start()

    stage_a(0)
    stage_a(1)
    stage_b(0)
    stage_c(0)
    stage_a(2)
    stage_d(0)
    max_ref[...] = fill(0, 0, s_a)

    def one_head(h, carry):
        last = LH - 1

        @pl.when(h < last)
        def _():
            stage_b(h + 1)

        step(h, 0, s_a, s_b, h, 1)

        @pl.when(h + 3 <= last)
        def _():
            stage_a(h + 3)

        @pl.when(h > 0)
        def _():
            combine(h - 1)

        step(h, 1, s_b, s_a, h, 2)

        @pl.when(h < last)
        def _():
            stage_c(h + 1)

        step(h, 2, s_a, s_b, h, 3)

        @pl.when(h < last)
        def _():
            stage_d(h + 1)

        step(h, 3, s_b, s_a, jnp.minimum(h + 1, last), 0)
        return carry

    lax.fori_loop(0, LH, one_head, 0)
    combine(LH - 1)

    def arrive(h, carry):
        for d in (1, 2, 3):
            hi(h, d, (z - d) % 4).wait_recv()
            ht(h, d, (z - d) % 4).wait_recv()
        hl(h, 0).wait()
        hl(h, 1).wait()
        return carry

    lax.fori_loop(0, LH, arrive, 0)
    r8 = lax.broadcasted_iota(jnp.int32, (8, tr), 0)
    c8 = lax.broadcasted_iota(jnp.int32, (8, tr), 1)
    mine = jnp.where(c8 == r8 + z * trows, 1.0, 0.0).astype(BF)
    out_txt[...] = dot(mine, txt_land[...], ((1,), (0,)))[:trows].astype(BF)

    def sent(h, carry):
        for d in (1, 2, 3):
            zkv(h, d, z).wait_send()
            zq(h, d, z).wait_send()
            yq(h, d, y).wait_send()
            hi(h, d, z).wait_send()
            ht(h, d, z).wait_send()
            yo(h, d - 1).wait_send()
            yl(h, d - 1).wait_send()
        for i in (0, 1):
            xs(h, i, own).wait_send()
            xf(h, i, own).wait_send()
        for i in range(4):
            sb(h, i, own).wait_send()
        return carry

    lax.fori_loop(0, LH, sent, 0)
    for d in (1, 2, 3):
        zt(d, z).wait_send()


def local(img_qkv, txt_qkv, q_gain, k_gain):
    rows, trows = img_qkv.shape[0], txt_qkv.shape[0]
    width = HEADS * HD
    blk_rows = GROUPS * (rows + trows)
    n_keys = 8 * blk_rows
    pad = -(-3 * LH * trows // 16) * 16
    gains = jnp.concatenate([q_gain[None], k_gain[None], jnp.zeros((6, HD), F32)], axis=0)
    frame_pairs = HD // 16
    side_pairs = (HD // 2 - frame_pairs) // 2
    freqs = jnp.concatenate(
        [axis_freqs(frame_pairs), axis_freqs(side_pairs), axis_freqs(side_pairs)]
    )
    freqs = jnp.broadcast_to(jnp.repeat(freqs, 2)[None, :], (8, HD))
    dma = pltpu.SemaphoreType.DMA
    vm = pltpu.VMEM
    return pl.pallas_call(
        kernel,
        out_shape=(
            jax.ShapeDtypeStruct((rows, width), BF),
            jax.ShapeDtypeStruct((trows, width), BF),
        ),
        in_specs=[pl.BlockSpec(memory_space=pltpu.VMEM)] * 4,
        out_specs=(pl.BlockSpec(memory_space=pltpu.VMEM),) * 2,
        scratch_shapes=[
            vm((GROUPS, LH, 2, rows, HD), BF),
            vm((GROUPS, LH, rows, HD), BF),
            vm((GROUPS, pad, HD), F32),
            vm((GROUPS, pad, HD), BF),
            vm((GROUPS, pad, HD), BF),
            vm((LH, 2, n_keys, HD), BF),
            vm((LH, 4, blk_rows, HD), BF),
            vm((blk_rows, n_keys), F32),
            vm((blk_rows, n_keys), F32),
            vm((LH, 3, blk_rows, HD), BF),
            vm((LH, 3, 8, HD), F32),
            vm((LH, 3, blk_rows, HD), BF),
            vm((LH, 3, 8, HD), F32),
            vm((blk_rows, HD), BF),
            vm((blk_rows, HD), F32),
            vm((LH, blk_rows, HD), BF),
            vm((GROUPS * trows, width), BF),
            vm((2, rows, HD), F32),
            vm((blk_rows, HD), F32),
            dma((LH, 2)), dma,
            dma((LH, 3)), dma((LH, 3)), dma((LH, 3)), dma((LH, 3)), dma((3,)), dma((3,)),
            dma((LH, 2)), dma((LH, 2)), dma((LH, 2)), dma((LH, 2)),
            dma((LH, 4)), dma((LH, 4)),
            dma((LH, 3)), dma((LH, 3)), dma((LH, 3)), dma((LH, 3)), dma((LH, 3)), dma((LH, 3)),
            dma((LH, 3)), dma((LH, 3)), dma((LH, 3)), dma((LH, 3)), dma((LH, 2)),
        ],
        compiler_params=pltpu.CompilerParams(
            collective_id=0, has_side_effects=True, vmem_limit_bytes=56 * 2**20
        ),
        cost_estimate=pl.CostEstimate(
            flops=4 * LH * 4 * blk_rows * n_keys * HD,
            bytes_accessed=4 * rows * 3 * width,
            transcendentals=LH * 4 * blk_rows * n_keys,
        ),
    )(img_qkv, txt_qkv, gains, freqs)


def solution(mesh):
    in_specs = (P(("blk", "head"), None), P(("blk", "head"), None), P(), P())
    out_specs = (P(("blk", "head"), None), P(("blk", "head"), None))
    return jax.shard_map(local, mesh=mesh, in_specs=in_specs, out_specs=out_specs, check_vma=False)
```

```python
import jax
import jax.numpy as jnp
import numpy as np
from jax import lax
from jax.experimental import pallas as pl
from jax.experimental.pallas import tpu as pltpu
from jax.sharding import PartitionSpec as P

HEADS = 24
HD = 128
GRID_W = 128
EPSILON = 1e-06
ZS = 4
GROUPS = 2 * ZS
LH = HEADS // GROUPS
MESH = pl.DeviceIdType.MESH
LOG2E = 1.4426950408889634
BF = jnp.bfloat16
F32 = jnp.float32


def dot(a, b, dims):
    return lax.dot_general(a, b, (dims, ((), ())), preferred_element_type=jnp.float32)


def freq_row():
    frame_pairs = HD // 16
    side_pairs = (HD // 2 - frame_pairs) // 2
    pair = lax.broadcasted_iota(jnp.int32, (1, HD), 1) // 2
    row = jnp.zeros((1, HD), F32)
    starts = ((0, frame_pairs), (frame_pairs, side_pairs), (frame_pairs + side_pairs, side_pairs))
    for start, count in starts:
        for k in range(count):
            row = jnp.where(pair == start + k, float(np.float32(10000.0 ** (-k / count))), row)
    return row


def kernel(
    img_hbm, txt_ref, qg_ref, kg_ref, out_img, out_txt,
    img_ref, kv_send, q_send, tx_f32, tx_send, tx_land, kv_all, q_all, s_a, s_b,
    acc_ref, m_ref, o_send, l_send, o_land, l_land, o_own, l_own, result, txt_land,
    cs_ref, max_ref,
    in_sem, zkv_r, zq_r, zt_r, xs_r, xf_r, so_r, sb_r, yq_r, yo_r, yl_r, hi_r, ht_r, send_sem,
):
    rows = img_ref.shape[0]
    trows = txt_ref.shape[0]
    blk_rows = ZS * (rows + trows)
    img_part = ZS * rows
    tr = ZS * trows
    width = HEADS * HD
    blk = lax.axis_index("blk")
    head = lax.axis_index("head")
    y = blk // 8
    x = ((blk // 4) % 2) * 2 + head // 2
    z = blk % 4
    c = head % 2
    y_pair = y + 1 - 2 * (y % 2)
    y_mate = 3 - y

    def al(v, n):
        return pl.multiple_of(v, n)

    def at(xx, yy, zz, cc):
        return (yy * 8 + ((xx % 4) // 2) * 4 + zz % 4, (xx % 2) * 2 + cc)

    def group(yy, zz):
        return (zz % 4) * 2 + ((yy + 1) // 2) % 2

    def ys(dy):
        return y if dy == 0 else y_pair

    others = [(0, 1), (0, 2), (0, 3), (1, 0), (1, 1), (1, 2), (1, 3)]

    loads = [
        pltpu.make_async_copy(
            img_hbm.at[:, pl.ds(p * width, width)], img_ref.at[:, pl.ds(p * width, width)], in_sem.at[p]
        )
        for p in range(3)
    ]
    for p in (1, 2, 0):
        loads[p].start()

    partners = [at(x, ys(dy), z + d, c) for dy, d in others]
    partners += [at(x, y_mate, z, c)]
    partners += [at(x + 1, y, z, c), at(x + 3, y, z, c), at(x, y, z, 1 - c)]
    barrier = pltpu.get_barrier_semaphore()
    for p in partners:
        pl.semaphore_signal(barrier, inc=1, device_id=p, device_id_type=MESH)

    def rc(src, dst, ss, rs, to):
        return pltpu.make_async_remote_copy(
            src_ref=src, dst_ref=dst, send_sem=ss, recv_sem=rs, device_id=to, device_id_type=MESH
        )

    zkv_s, zq_s, zt_s, xs_s, xf_s, sb_s, yq_s, yo_s, yl_s, hi_s, ht_s = (
        send_sem.at[i] for i in range(11)
    )
    side = 4 * blk_rows
    OWN, RIGHT, FAR, LEFT = (i * blk_rows for i in range(4))

    def kv_rows(h, jj, start, n):
        return kv_all.at[h, jj, :, pl.ds(start, n), :]

    def landed(ref, sem):
        pltpu.make_async_copy(ref, ref, sem).wait()

    def zkv(h, dy, d):
        return rc(
            kv_send.at[group(ys(dy), z + d), h],
            kv_rows(h, dy, al(z * rows, 16), rows),
            zkv_s, zkv_r.at[h, dy], at(x, ys(dy), z + d, c),
        )

    def zq(h, dy, d):
        return rc(
            q_send.at[group(ys(dy), z + d), h],
            q_all.at[h, dy, pl.ds(al(z * rows, 16), rows), :],
            zq_s, zq_r.at[h], at(x, ys(dy), z + d, c),
        )

    def zt(dy, d):
        return rc(
            tx_send.at[group(ys(dy), z + d)], tx_land.at[dy, z],
            zt_s, zt_r, at(x, ys(dy), z + d, c),
        )

    def lkv(h):
        return pltpu.make_async_copy(
            kv_send.at[group(y, z), h], kv_rows(h, 0, al(z * rows, 16), rows), zkv_r.at[h, 0]
        )

    def lq(h):
        return pltpu.make_async_copy(
            q_send.at[group(y, z), h],
            q_all.at[h, 0, pl.ds(al(z * rows, 16), rows), :],
            zq_r.at[h],
        )

    def xs(h, jj, i):
        return rc(
            kv_rows(h, jj, OWN, blk_rows),
            kv_rows(h, jj, LEFT if i == 0 else RIGHT, blk_rows),
            xs_s, xs_r.at[h, jj, i], at(x + (1 if i == 0 else 3), y, z, c),
        )

    def xf(h, jj, i):
        return rc(
            kv_all.at[h, jj, i, pl.ds(LEFT if i == 0 else RIGHT, blk_rows), :],
            kv_all.at[h, jj, i, pl.ds(FAR, blk_rows), :],
            xf_s, xf_r.at[h, jj], at(x + (1 if i == 0 else 3), y, z, c),
        )

    def sb(h, jj, which):
        return rc(
            kv_rows(h, jj, which, blk_rows),
            kv_rows(h, jj, side + which, blk_rows),
            sb_s, so_r.at[h] if which == OWN else sb_r.at[h, jj], at(x, y, z, 1 - c),
        )

    def yq(h):
        return rc(
            q_all.at[h, pl.ds(0, 2)], q_all.at[h, pl.ds(2, 2)],
            yq_s, yq_r.at[h], at(x, y_mate, z, c),
        )

    def yo(h, b):
        return rc(o_send.at[h, b], o_land.at[h, b], yo_s, yo_r.at[h, b], at(x, y_mate, z, c))

    def yl(h, b):
        return rc(l_send.at[h, b], l_land.at[h, b], yl_s, yl_r.at[h, b], at(x, y_mate, z, c))

    def lanes_of(h, g):
        return pl.ds(al((g * LH + h) * HD, HD), HD)

    def hi(h, dy, d, g):
        return rc(
            result.at[h, dy, pl.ds(al(((z + d) % 4) * rows, 16), rows), :],
            out_img.at[:, lanes_of(h, g)],
            hi_s, hi_r, at(x, ys(dy), z + d, c),
        )

    def ht(h, dy, d, g):
        return rc(
            result.at[h, dy, pl.ds(img_part, tr), :],
            txt_land.at[:, lanes_of(h, g)],
            ht_s, ht_r, at(x, ys(dy), z + d, c),
        )

    def hl(h, i):
        lanes = lanes_of(h, group(y, z))
        if i == 0:
            src, dst = result.at[h, 0, pl.ds(al(z * rows, 16), rows), :], out_img.at[:, lanes]
            return pltpu.make_async_copy(src, dst, hi_r)
        src, dst = result.at[h, 0, pl.ds(img_part, tr), :], txt_land.at[:, lanes]
        return pltpu.make_async_copy(src, dst, ht_r)

    device = blk * 4 + head
    half_devices = 64
    lane = lax.broadcasted_iota(jnp.int32, (rows, HD), 1)
    pair = lane // 2
    within = (device % half_devices) * rows + lax.broadcasted_iota(jnp.int32, (rows, HD), 0)
    frame_pairs = HD // 16
    side_pairs = (HD // 2 - frame_pairs) // 2
    frame_pos = jnp.full((rows, HD), device // half_devices, jnp.int32)
    position = jnp.where(
        pair < frame_pairs,
        frame_pos,
        jnp.where(pair < frame_pairs + side_pairs, within // GRID_W, within % GRID_W),
    )
    angles = position.astype(F32) * freq_row()
    cs_ref[0] = jnp.cos(angles)
    cs_ref[1] = jnp.where(lane % 2 == 0, -1.0, 1.0) * jnp.sin(angles)

    def normal(v, gain):
        return v * lax.rsqrt(jnp.mean(v * v, axis=-1, keepdims=True) + EPSILON) * gain

    def rope(v):
        even = lax.broadcasted_iota(jnp.int32, v.shape, 1) % 2 == 0
        swapped = jnp.where(even, pltpu.roll(v, HD - 1, 1), pltpu.roll(v, 1, 1))
        return cs_ref[0] * v + cs_ref[1] * swapped

    def prep_kv(h):
        for g in range(GROUPS):
            base = (g * LH + h) * HD
            k = img_ref[:, width + base : width + base + HD].astype(F32)
            kv_send[g, h, 0] = rope(normal(k, kg_ref[...])).astype(BF)
            kv_send[g, h, 1] = img_ref[:, 2 * width + base : 2 * width + base + HD]

    def prep_q(h):
        for g in range(GROUPS):
            base = (g * LH + h) * HD
            q = img_ref[:, base : base + HD].astype(F32)
            q_send[g, h] = rope(normal(q, qg_ref[...])).astype(BF)

    def send_kv(h, dys):
        for dy, d in others:
            if dy in dys:
                zkv(h, dy, d).start()
        if 0 in dys:
            lkv(h).start()

    def send_q(h):
        for dy, d in others:
            zq(h, dy, d).start()
        lq(h).start()

    def prep_text():
        for g in range(GROUPS):
            for part, gain in ((0, qg_ref), (1, kg_ref), (2, None)):
                for h in range(LH):
                    lo = part * width + (g * LH + h) * HD
                    v = txt_ref[:, lo : lo + HD].astype(F32)
                    if gain is not None:
                        v = normal(v, gain[...])
                    r = (part * LH + h) * trows
                    tx_f32[g, r : r + trows, :] = v
            used = 3 * LH * trows
            tx_f32[g, used:, :] = jnp.zeros((tx_f32.shape[1] - used, HD), F32)
            tx_send[g] = tx_f32[g].astype(BF)

    def send_text():
        for dy, d in others:
            zt(dy, d).start()
        pltpu.make_async_copy(tx_send.at[group(y, z)], tx_land.at[0, z], zt_r).start()

    def place_text():
        landed(tx_land, zt_r)
        pad = tx_land.shape[2]
        row = lax.broadcasted_iota(jnp.int32, (tr, ZS * pad), 0)
        col = lax.broadcasted_iota(jnp.int32, (tr, ZS * pad), 1)
        target = (row // trows) * pad + row % trows
        pick = jnp.concatenate(
            [jnp.where(col == target + j * trows, 1.0, 0.0).astype(BF) for j in range(3 * LH)],
            axis=0,
        )
        for jj in range(2):
            texts = dot(pick, tx_land[jj].reshape(ZS * pad, HD), ((1,), (0,))).astype(BF)
            for h in range(LH):
                q_all[h, jj, img_part:, :] = texts[h * tr : (h + 1) * tr]
                for part in (0, 1):
                    r = ((part + 1) * LH + h) * tr
                    kv_all[h, jj, part, img_part:blk_rows, :] = texts[r : r + tr]

    def stage_a(h, jj):
        landed(kv_rows(h, jj, 0, img_part), zkv_r.at[h, jj])
        sb(h, jj, OWN).start()

    def stage_x(h, jj):
        xs(h, jj, 0).start()
        xs(h, jj, 1).start()

    def stage_b(h, jj):
        landed(kv_rows(h, jj, LEFT, blk_rows), xs_r.at[h, jj, 0])
        xf(h, jj, 0).start()
        landed(kv_rows(h, jj, RIGHT, blk_rows), xs_r.at[h, jj, 1])
        xf(h, jj, 1).start()
        sb(h, jj, LEFT).start()
        sb(h, jj, RIGHT).start()

    def stage_c(h, jj):
        landed(kv_rows(h, jj, FAR, blk_rows), xf_r.at[h, jj])
        sb(h, jj, FAR).start()

    def stage_d(h, jj):
        landed(kv_rows(h, jj, side + RIGHT, 3 * blk_rows), sb_r.at[h, jj])

    def stage_own(h):
        landed(kv_all.at[h, :, :, pl.ds(side, blk_rows), :], so_r.at[h])

    def share_q(h):
        landed(q_all.at[h, pl.ds(0, 2), pl.ds(0, img_part), :], zq_r.at[h])
        yq(h).start()

    scale = LOG2E * HD**-0.5

    def fill(h, unit, b, s_ref):
        q = q_all[h, b].astype(F32) * scale
        high = q.astype(BF)
        low = (q - high.astype(F32)).astype(BF)
        k = kv_all[h, unit, 0]
        n = k.shape[0]
        s = dot(
            jnp.concatenate([high, low], axis=1), jnp.concatenate([k, k], axis=1), ((1,), (1,))
        )
        s_ref[...] = s
        top = s[:, 0:HD]
        for t in range(1, n // HD):
            top = jnp.maximum(top, s[:, t * HD : (t + 1) * HD])
        top = jnp.max(top, axis=1, keepdims=True)
        max_ref[...] = jnp.broadcast_to(top, (blk_rows, HD))

    eye = lax.broadcasted_iota(jnp.int32, (HD, HD), 0) == lax.broadcasted_iota(
        jnp.int32, (HD, HD), 1
    )

    def rows_to_lanes(v):
        lines = []
        for r in range(0, blk_rows, HD):
            n = min(HD, blk_rows - r)
            lines.append(jnp.sum(jnp.where(eye[:n], v[r : r + n], 0.0), axis=0, keepdims=True))
        lines.append(jnp.zeros((8 - len(lines), HD), F32))
        return jnp.concatenate(lines, axis=0)

    def lanes_to_rows(v):
        parts = []
        for j, r in enumerate(range(0, blk_rows, HD)):
            n = min(HD, blk_rows - r)
            line = jnp.broadcast_to(v[j : j + 1], (n, HD))
            parts.append(jnp.sum(jnp.where(eye[:n], line, 0.0), axis=1, keepdims=True))
        return jnp.concatenate(parts, axis=0)

    def step(h, unit, b, s_in, s_out, after):
        first, final = unit == 0, unit == 1
        m = max_ref[...]
        if not first:
            before = m_ref[b]
            m = jnp.maximum(before, m)
        v = kv_all[h, unit, 1]
        n = v.shape[0]
        ps = []
        for lo in range(0, n, HD):
            ps.append(jnp.exp2(s_in[:, lo : lo + HD] - m).astype(BF))
        if after is not None:
            fill(*after, s_out)
        p = jnp.concatenate(ps, axis=1)
        acc = dot(p, jnp.concatenate([v, jnp.ones_like(v)], axis=1), ((1,), (0,)))
        out, total = acc[:, :HD], acc[:, HD:]
        if not first:
            w = jnp.exp2(before - m)
            out = out + acc_ref[b, :, :HD] * w
            total = total + acc_ref[b, :, HD:] * w
        if not final:
            acc_ref[b, :, :HD] = out
            acc_ref[b, :, HD:] = total
            m_ref[b] = m
            return
        o = (out / total).astype(BF)
        lse = m + jnp.log2(total)
        if b >= 2:
            o_send[h, b - 2] = o
            l_send[h, b - 2] = rows_to_lanes(lse)
            yo(h, b - 2).start()
            yl(h, b - 2).start()
        else:
            o_own[h, b] = o
            l_own[h, b] = lse

    def combine(h, dy):
        yo(h, dy).wait_recv()
        yl(h, dy).wait_recv()
        mine, theirs = l_own[h, dy], lanes_to_rows(l_land[h, dy])
        top = jnp.maximum(mine, theirs)
        w0, w1 = jnp.exp2(mine - top), jnp.exp2(theirs - top)
        o = o_own[h, dy].astype(F32) * w0 + o_land[h, dy].astype(F32) * w1
        result[h, dy] = (o / (w0 + w1)).astype(BF)
        g = group(y, z)
        for e, d in others:
            if e == dy:
                hi(h, dy, d, g).start()
                ht(h, dy, d, g).start()
        if dy == 0:
            hl(h, 0).start()
            hl(h, 1).start()

    prep_text()
    loads[1].wait()
    loads[2].wait()
    prep_kv(0)
    pl.semaphore_wait(barrier, len(partners))
    send_text()
    send_kv(0, (0,))
    loads[0].wait()
    prep_q(0)
    send_kv(0, (1,))
    prep_kv(1)
    place_text()
    stage_a(0, 0)
    stage_x(0, 0)
    send_q(0)
    prep_q(1)
    stage_a(0, 1)
    stage_x(0, 1)
    send_kv(1, (0, 1))
    share_q(0)
    send_q(1)
    prep_kv(2)
    stage_b(0, 0)
    prep_q(2)
    stage_c(0, 0)
    stage_a(1, 0)
    stage_b(0, 1)
    stage_x(1, 0)
    stage_own(0)
    stage_d(0, 0)

    plan = [(0, 0, b) for b in (0, 1, 2, 3)]
    plan += [(0, 1, b) for b in (2, 3, 0, 1)]
    plan += [(1, 0, b) for b in (0, 1, 2, 3)]
    plan += [(1, 1, b) for b in (2, 3, 0, 1)]
    plan += [(2, 0, 2), (2, 0, 3), (2, 1, 2), (2, 1, 3)]
    plan += [(2, 0, 0), (2, 1, 0), (2, 0, 1), (2, 1, 1)]

    def head_q(h):
        yq(h).wait_recv()

    before_step = {
        0: [(send_kv, 2, (0, 1))],
        1: [(head_q, 0), (send_q, 2)],
        2: [(stage_c, 0, 1), (stage_a, 1, 1), (stage_x, 1, 1)],
        3: [(stage_b, 1, 0), (stage_d, 0, 1)],
        4: [(share_q, 1)],
        5: [(stage_a, 2, 0), (stage_x, 2, 0)],
        6: [(stage_c, 1, 0), (stage_b, 1, 1)],
        7: [(stage_own, 1), (stage_d, 1, 0)],
        8: [(stage_a, 2, 1), (stage_x, 2, 1)],
        9: [(stage_c, 1, 1), (stage_b, 2, 0), (head_q, 1), (combine, 0, 0)],
        10: [(share_q, 2), (combine, 0, 1)],
        11: [(stage_d, 1, 1)],
        12: [(stage_c, 2, 0)],
        13: [(stage_b, 2, 1)],
        15: [(stage_c, 2, 1), (stage_own, 2), (stage_d, 2, 0), (head_q, 2)],
        16: [(combine, 1, 0)],
        17: [(stage_d, 2, 1), (combine, 1, 1)],
        22: [(combine, 2, 0)],
    }
    bufs = (s_a, s_b)
    fill(*plan[0], s_a)
    for t, (h, unit, b) in enumerate(plan):
        for act, *args in before_step.get(t, ()):
            act(*args)
        after = plan[t + 1] if t + 1 < len(plan) else None
        step(h, unit, b, bufs[t % 2], bufs[(t + 1) % 2], after)
    combine(2, 1)

    landed(txt_land, ht_r)
    r8 = lax.broadcasted_iota(jnp.int32, (8, tr), 0)
    c8 = lax.broadcasted_iota(jnp.int32, (8, tr), 1)
    mine = jnp.where(c8 == r8 + z * trows, 1.0, 0.0).astype(BF)
    out_txt[...] = dot(mine, txt_land[...], ((1,), (0,)))[:trows].astype(BF)

    landed(out_img, hi_r)
    landed(kv_send.at[pl.ds(0, len(others))], zkv_s)
    landed(q_send.at[pl.ds(0, len(others))], zq_s)
    landed(tx_send.at[pl.ds(0, len(others))], zt_s)
    landed(kv_all.at[:, :, :, pl.ds(0, 2 * blk_rows), :], xs_s)
    landed(kv_all.at[:, :, :, pl.ds(0, blk_rows), :], xf_s)
    landed(kv_all.at[:, :, :, pl.ds(0, side), :], sb_s)
    landed(q_all.at[:, pl.ds(0, 2)], yq_s)
    landed(o_send, yo_s)
    landed(l_send, yl_s)
    landed(q_send.at[pl.ds(0, len(others))], hi_s)
    landed(result.at[0, 0, pl.ds(0, LH * len(others) * tr), :], ht_s)


def local(img_qkv, txt_qkv, q_gain, k_gain):
    rows, trows = img_qkv.shape[0], txt_qkv.shape[0]
    width = HEADS * HD
    blk_rows = ZS * (rows + trows)
    n_keys = 8 * blk_rows
    pad = -(-3 * LH * trows // 16) * 16
    dma = pltpu.SemaphoreType.DMA
    vm = pltpu.VMEM
    return pl.pallas_call(
        kernel,
        out_shape=(
            jax.ShapeDtypeStruct((rows, width), BF),
            jax.ShapeDtypeStruct((trows, width), BF),
        ),
        in_specs=[pl.BlockSpec(memory_space=pl.ANY)]
        + [pl.BlockSpec(memory_space=pltpu.VMEM)] * 3,
        out_specs=(pl.BlockSpec(memory_space=pl.ANY), pl.BlockSpec(memory_space=pltpu.VMEM)),
        scratch_shapes=[
            vm((rows, 3 * width), BF),
            vm((GROUPS, LH, 2, rows, HD), BF),
            vm((GROUPS, LH, rows, HD), BF),
            vm((GROUPS, pad, HD), F32),
            vm((GROUPS, pad, HD), BF),
            vm((2, ZS, pad, HD), BF),
            vm((LH, 2, 2, n_keys, HD), BF),
            vm((LH, 4, blk_rows, HD), BF),
            vm((blk_rows, n_keys), F32),
            vm((blk_rows, n_keys), F32),
            vm((4, blk_rows, 2 * HD), F32),
            vm((4, blk_rows, HD), F32),
            vm((LH, 2, blk_rows, HD), BF),
            vm((LH, 2, 8, HD), F32),
            vm((LH, 2, blk_rows, HD), BF),
            vm((LH, 2, 8, HD), F32),
            vm((LH, 2, blk_rows, HD), BF),
            vm((LH, 2, blk_rows, HD), F32),
            vm((LH, 2, blk_rows, HD), BF),
            vm((ZS * trows, width), BF),
            vm((2, rows, HD), F32),
            vm((blk_rows, HD), F32),
            dma((3,)), dma((LH, 2)), dma((LH,)), dma, dma((LH, 2, 2)), dma((LH, 2)),
            dma((LH,)), dma((LH, 2)), dma((LH,)), dma((LH, 2)), dma((LH, 2)), dma, dma, dma((11,)),
        ],
        compiler_params=pltpu.CompilerParams(
            collective_id=0, has_side_effects=True, vmem_limit_bytes=56 * 2**20
        ),
        cost_estimate=pl.CostEstimate(
            flops=4 * LH * 8 * blk_rows * n_keys * HD,
            bytes_accessed=4 * rows * 3 * width,
            transcendentals=LH * 8 * blk_rows * n_keys,
        ),
    )(img_qkv, txt_qkv, q_gain.reshape(1, HD), k_gain.reshape(1, HD))


def solution(mesh):
    in_specs = (P(("blk", "head"), None), P(("blk", "head"), None), P(), P())
    out_specs = (P(("blk", "head"), None), P(("blk", "head"), None))
    return jax.shard_map(local, mesh=mesh, in_specs=in_specs, out_specs=out_specs, check_vma=False)
```

```python
import jax
import jax.numpy as jnp
import numpy as np
from jax import lax
from jax.experimental import pallas as pl
from jax.experimental.pallas import tpu as pltpu
from jax.sharding import PartitionSpec as P

HEADS = 24
HD = 128
GRID_W = 128
EPSILON = 1e-06
ZS = 4
GROUPS = 2 * ZS
LH = HEADS // GROUPS
MESH = pl.DeviceIdType.MESH
LOG2E = 1.4426950408889634
BF = jnp.bfloat16
F32 = jnp.float32


def dot(a, b, dims):
    return lax.dot_general(a, b, (dims, ((), ())), preferred_element_type=jnp.float32)


def freq_row():
    frame_pairs = HD // 16
    side_pairs = (HD // 2 - frame_pairs) // 2
    pair = lax.broadcasted_iota(jnp.int32, (1, HD), 1) // 2
    row = jnp.zeros((1, HD), F32)
    starts = ((0, frame_pairs), (frame_pairs, side_pairs), (frame_pairs + side_pairs, side_pairs))
    for start, count in starts:
        for k in range(count):
            row = jnp.where(pair == start + k, float(np.float32(10000.0 ** (-k / count))), row)
    return row


def kernel(
    img_hbm, txt_ref, qg_ref, kg_ref, out_img, out_txt,
    img_ref, kv_send, q_send, tx_f32, tx_send, tx_land, kv_all, q_all, s_a, s_b,
    acc_ref, m_ref, o_send, l_send, o_land, l_land, o_own, l_own, result, txt_land,
    cs_ref, max_ref,
    in_sem, zkv_r, zq_r, zt_r, xs_r, xf_r, so_r, sb_r, yq_r, yo_r, yl_r, hi_r, ht_r, send_sem,
):
    rows = img_ref.shape[0]
    trows = txt_ref.shape[0]
    blk_rows = ZS * (rows + trows)
    img_part = ZS * rows
    tr = ZS * trows
    width = HEADS * HD
    blk = lax.axis_index("blk")
    head = lax.axis_index("head")
    y = blk // 8
    x = ((blk // 4) % 2) * 2 + head // 2
    z = blk % 4
    c = head % 2
    y_pair = y + 1 - 2 * (y % 2)
    y_mate = 3 - y

    def al(v, n):
        return pl.multiple_of(v, n)

    def at(xx, yy, zz, cc):
        return (yy * 8 + ((xx % 4) // 2) * 4 + zz % 4, (xx % 2) * 2 + cc)

    def group(yy, zz):
        return (zz % 4) * 2 + ((yy + 1) // 2) % 2

    def ys(dy):
        return y if dy == 0 else y_pair

    others = [(0, 1), (0, 2), (0, 3), (1, 0), (1, 1), (1, 2), (1, 3)]

    loads = [
        pltpu.make_async_copy(
            img_hbm.at[:, pl.ds(p * width, width)], img_ref.at[:, pl.ds(p * width, width)], in_sem.at[p]
        )
        for p in range(3)
    ]
    for p in (1, 2, 0):
        loads[p].start()

    partners = [at(x, ys(dy), z + d, c) for dy, d in others]
    partners += [at(x, y_mate, z, c)]
    partners += [at(x + 1, y, z, c), at(x + 3, y, z, c), at(x, y, z, 1 - c)]
    barrier = pltpu.get_barrier_semaphore()
    for p in partners:
        pl.semaphore_signal(barrier, inc=1, device_id=p, device_id_type=MESH)

    def rc(src, dst, ss, rs, to):
        return pltpu.make_async_remote_copy(
            src_ref=src, dst_ref=dst, send_sem=ss, recv_sem=rs, device_id=to, device_id_type=MESH
        )

    zkv_s, zq_s, zt_s, xs_s, xf_s, sb_s, yq_s, yo_s, yl_s, hi_s, ht_s = (
        send_sem.at[i] for i in range(11)
    )
    side = 4 * blk_rows
    OWN, RIGHT, FAR, LEFT = (i * blk_rows for i in range(4))

    def kv_rows(h, jj, start, n):
        return kv_all.at[h, jj, :, pl.ds(start, n), :]

    def landed(ref, sem):
        pltpu.make_async_copy(ref, ref, sem).wait()

    def zkv(h, dy, d):
        return rc(
            kv_send.at[group(ys(dy), z + d), h],
            kv_rows(h, dy, al(z * rows, 16), rows),
            zkv_s, zkv_r.at[h, dy], at(x, ys(dy), z + d, c),
        )

    def zq(h, dy, d):
        return rc(
            q_send.at[group(ys(dy), z + d), h],
            q_all.at[h, dy, pl.ds(al(z * rows, 16), rows), :],
            zq_s, zq_r.at[h], at(x, ys(dy), z + d, c),
        )

    def zt(dy, d):
        return rc(
            tx_send.at[group(ys(dy), z + d)], tx_land.at[dy, z],
            zt_s, zt_r, at(x, ys(dy), z + d, c),
        )

    def lkv(h):
        return pltpu.make_async_copy(
            kv_send.at[group(y, z), h], kv_rows(h, 0, al(z * rows, 16), rows), zkv_r.at[h, 0]
        )

    def lq(h):
        return pltpu.make_async_copy(
            q_send.at[group(y, z), h],
            q_all.at[h, 0, pl.ds(al(z * rows, 16), rows), :],
            zq_r.at[h],
        )

    def xs(h, jj, i):
        return rc(
            kv_rows(h, jj, OWN, blk_rows),
            kv_rows(h, jj, LEFT if i == 0 else RIGHT, blk_rows),
            xs_s, xs_r.at[h, jj, i], at(x + (1 if i == 0 else 3), y, z, c),
        )

    def xf(h, jj, i):
        return rc(
            kv_all.at[h, jj, i, pl.ds(LEFT if i == 0 else RIGHT, blk_rows), :],
            kv_all.at[h, jj, i, pl.ds(FAR, blk_rows), :],
            xf_s, xf_r.at[h, jj], at(x + (1 if i == 0 else 3), y, z, c),
        )

    def sb(h, jj, which):
        return rc(
            kv_rows(h, jj, which, blk_rows),
            kv_rows(h, jj, side + which, blk_rows),
            sb_s, so_r.at[h] if which == OWN else sb_r.at[h, jj], at(x, y, z, 1 - c),
        )

    def yq(h):
        return rc(
            q_all.at[h, pl.ds(0, 2)], q_all.at[h, pl.ds(2, 2)],
            yq_s, yq_r.at[h], at(x, y_mate, z, c),
        )

    def yo(h, b):
        return rc(o_send.at[h, b], o_land.at[h, b], yo_s, yo_r.at[h, b], at(x, y_mate, z, c))

    def yl(h, b):
        return rc(l_send.at[h, b], l_land.at[h, b], yl_s, yl_r.at[h, b], at(x, y_mate, z, c))

    def lanes_of(h, g):
        return pl.ds(al((g * LH + h) * HD, HD), HD)

    def hi(h, dy, d, g):
        return rc(
            result.at[h, dy, pl.ds(al(((z + d) % 4) * rows, 16), rows), :],
            out_img.at[:, lanes_of(h, g)],
            hi_s, hi_r, at(x, ys(dy), z + d, c),
        )

    def ht(h, dy, d, g):
        return rc(
            result.at[h, dy, pl.ds(img_part, tr), :],
            txt_land.at[:, lanes_of(h, g)],
            ht_s, ht_r, at(x, ys(dy), z + d, c),
        )

    def hl(h, i):
        lanes = lanes_of(h, group(y, z))
        if i == 0:
            src, dst = result.at[h, 0, pl.ds(al(z * rows, 16), rows), :], out_img.at[:, lanes]
            return pltpu.make_async_copy(src, dst, hi_r)
        src, dst = result.at[h, 0, pl.ds(img_part, tr), :], txt_land.at[:, lanes]
        return pltpu.make_async_copy(src, dst, ht_r)

    device = blk * 4 + head
    half_devices = 64
    lane = lax.broadcasted_iota(jnp.int32, (rows, HD), 1)
    pair = lane // 2
    within = (device % half_devices) * rows + lax.broadcasted_iota(jnp.int32, (rows, HD), 0)
    frame_pairs = HD // 16
    side_pairs = (HD // 2 - frame_pairs) // 2
    frame_pos = jnp.full((rows, HD), device // half_devices, jnp.int32)
    position = jnp.where(
        pair < frame_pairs,
        frame_pos,
        jnp.where(pair < frame_pairs + side_pairs, within // GRID_W, within % GRID_W),
    )
    angles = position.astype(F32) * freq_row()
    cs_ref[0] = jnp.cos(angles)
    cs_ref[1] = jnp.where(lane % 2 == 0, -1.0, 1.0) * jnp.sin(angles)

    def normal(v, gain):
        return v * lax.rsqrt(jnp.mean(v * v, axis=-1, keepdims=True) + EPSILON) * gain

    def rope(v):
        even = lax.broadcasted_iota(jnp.int32, v.shape, 1) % 2 == 0
        swapped = jnp.where(even, pltpu.roll(v, HD - 1, 1), pltpu.roll(v, 1, 1))
        return cs_ref[0] * v + cs_ref[1] * swapped

    def prep_kv(h):
        for g in range(GROUPS):
            base = (g * LH + h) * HD
            k = img_ref[:, width + base : width + base + HD].astype(F32)
            kv_send[g, h, 0] = rope(normal(k, kg_ref[...])).astype(BF)
            kv_send[g, h, 1] = img_ref[:, 2 * width + base : 2 * width + base + HD]

    def prep_q(h):
        for g in range(GROUPS):
            base = (g * LH + h) * HD
            q = img_ref[:, base : base + HD].astype(F32)
            q_send[g, h] = rope(normal(q, qg_ref[...])).astype(BF)

    def send_kv(h, dys):
        for dy, d in others:
            if dy in dys:
                zkv(h, dy, d).start()
        if 0 in dys:
            lkv(h).start()

    def send_q(h):
        for dy, d in others:
            zq(h, dy, d).start()
        lq(h).start()

    def prep_text():
        for g in range(GROUPS):
            for part, gain in ((0, qg_ref), (1, kg_ref), (2, None)):
                for h in range(LH):
                    lo = part * width + (g * LH + h) * HD
                    v = txt_ref[:, lo : lo + HD].astype(F32)
                    if gain is not None:
                        v = normal(v, gain[...])
                    r = (part * LH + h) * trows
                    tx_f32[g, r : r + trows, :] = v
            used = 3 * LH * trows
            tx_f32[g, used:, :] = jnp.zeros((tx_f32.shape[1] - used, HD), F32)
            tx_send[g] = tx_f32[g].astype(BF)

    def send_text():
        for dy, d in others:
            zt(dy, d).start()
        pltpu.make_async_copy(tx_send.at[group(y, z)], tx_land.at[0, z], zt_r).start()

    def place_text():
        landed(tx_land, zt_r)
        pad = tx_land.shape[2]
        row = lax.broadcasted_iota(jnp.int32, (tr, ZS * pad), 0)
        col = lax.broadcasted_iota(jnp.int32, (tr, ZS * pad), 1)
        target = (row // trows) * pad + row % trows
        pick = jnp.concatenate(
            [jnp.where(col == target + j * trows, 1.0, 0.0).astype(BF) for j in range(3 * LH)],
            axis=0,
        )
        for jj in range(2):
            texts = dot(pick, tx_land[jj].reshape(ZS * pad, HD), ((1,), (0,))).astype(BF)
            for h in range(LH):
                q_all[h, jj, img_part:, :] = texts[h * tr : (h + 1) * tr]
                for part in (0, 1):
                    r = ((part + 1) * LH + h) * tr
                    kv_all[h, jj, part, img_part:blk_rows, :] = texts[r : r + tr]

    def stage_a(h, jj):
        landed(kv_rows(h, jj, 0, img_part), zkv_r.at[h, jj])
        sb(h, jj, OWN).start()

    def stage_x(h, jj):
        xs(h, jj, 0).start()
        xs(h, jj, 1).start()

    def stage_b(h, jj):
        landed(kv_rows(h, jj, LEFT, blk_rows), xs_r.at[h, jj, 0])
        xf(h, jj, 0).start()
        landed(kv_rows(h, jj, RIGHT, blk_rows), xs_r.at[h, jj, 1])
        xf(h, jj, 1).start()
        sb(h, jj, LEFT).start()
        sb(h, jj, RIGHT).start()

    def stage_c(h, jj):
        landed(kv_rows(h, jj, FAR, blk_rows), xf_r.at[h, jj])
        sb(h, jj, FAR).start()

    def stage_d(h, jj):
        landed(kv_rows(h, jj, side + RIGHT, 3 * blk_rows), sb_r.at[h, jj])

    def stage_own(h):
        landed(kv_all.at[h, :, :, pl.ds(side, blk_rows), :], so_r.at[h])

    def share_q(h):
        landed(q_all.at[h, pl.ds(0, 2), pl.ds(0, img_part), :], zq_r.at[h])
        yq(h).start()

    scale = LOG2E * HD**-0.5

    def fill(h, unit, b, s_ref):
        q = q_all[h, b].astype(F32) * scale
        high = q.astype(BF)
        low = (q - high.astype(F32)).astype(BF)
        k = kv_all[h, unit, 0]
        n = k.shape[0]
        s = dot(
            jnp.concatenate([high, low], axis=1), jnp.concatenate([k, k], axis=1), ((1,), (1,))
        )
        s_ref[...] = s
        top = s[:, 0:HD]
        for t in range(1, n // HD):
            top = jnp.maximum(top, s[:, t * HD : (t + 1) * HD])
        top = jnp.max(top, axis=1, keepdims=True)
        max_ref[...] = jnp.broadcast_to(top, (blk_rows, HD))

    eye = lax.broadcasted_iota(jnp.int32, (HD, HD), 0) == lax.broadcasted_iota(
        jnp.int32, (HD, HD), 1
    )

    def rows_to_lanes(v):
        lines = []
        for r in range(0, blk_rows, HD):
            n = min(HD, blk_rows - r)
            lines.append(jnp.sum(jnp.where(eye[:n], v[r : r + n], 0.0), axis=0, keepdims=True))
        lines.append(jnp.zeros((8 - len(lines), HD), F32))
        return jnp.concatenate(lines, axis=0)

    def lanes_to_rows(v):
        parts = []
        for j, r in enumerate(range(0, blk_rows, HD)):
            n = min(HD, blk_rows - r)
            line = jnp.broadcast_to(v[j : j + 1], (n, HD))
            parts.append(jnp.sum(jnp.where(eye[:n], line, 0.0), axis=1, keepdims=True))
        return jnp.concatenate(parts, axis=0)

    def step(h, unit, b, s_in, s_out, after):
        first, final = unit == 0, unit == 1
        m = max_ref[...]
        if not first:
            before = m_ref[b]
            m = jnp.maximum(before, m)
        v = kv_all[h, unit, 1]
        n = v.shape[0]
        ps = []
        for lo in range(0, n, HD):
            ps.append(jnp.exp2(s_in[:, lo : lo + HD] - m).astype(BF))
        if after is not None:
            fill(*after, s_out)
        p = jnp.concatenate(ps, axis=1)
        acc = dot(p, jnp.concatenate([v, jnp.ones_like(v)], axis=1), ((1,), (0,)))
        out, total = acc[:, :HD], acc[:, HD:]
        if not first:
            w = jnp.exp2(before - m)
            out = out + acc_ref[b, :, :HD] * w
            total = total + acc_ref[b, :, HD:] * w
        if not final:
            acc_ref[b, :, :HD] = out
            acc_ref[b, :, HD:] = total
            m_ref[b] = m
            return
        o = (out / total).astype(BF)
        lse = m + jnp.log2(total)
        if b >= 2:
            o_send[h, b - 2] = o
            l_send[h, b - 2] = rows_to_lanes(lse)
            yo(h, b - 2).start()
            yl(h, b - 2).start()
        else:
            o_own[h, b] = o
            l_own[h, b] = lse

    def combine(h, dy):
        yo(h, dy).wait_recv()
        yl(h, dy).wait_recv()
        mine, theirs = l_own[h, dy], lanes_to_rows(l_land[h, dy])
        top = jnp.maximum(mine, theirs)
        w0, w1 = jnp.exp2(mine - top), jnp.exp2(theirs - top)
        o = o_own[h, dy].astype(F32) * w0 + o_land[h, dy].astype(F32) * w1
        result[h, dy] = (o / (w0 + w1)).astype(BF)
        g = group(y, z)
        for e, d in others:
            if e == dy:
                hi(h, dy, d, g).start()
                ht(h, dy, d, g).start()
        if dy == 0:
            hl(h, 0).start()
            hl(h, 1).start()

    prep_text()
    loads[1].wait()
    loads[2].wait()
    prep_kv(0)
    pl.semaphore_wait(barrier, len(partners))
    send_text()
    send_kv(0, (0,))
    loads[0].wait()
    prep_q(0)
    send_kv(0, (1,))
    prep_kv(1)
    place_text()
    stage_a(0, 0)
    stage_x(0, 0)
    send_q(0)
    prep_q(1)
    stage_a(0, 1)
    stage_x(0, 1)
    send_kv(1, (0, 1))
    stage_b(0, 0)
    share_q(0)
    send_q(1)
    prep_kv(2)
    prep_q(2)
    stage_c(0, 0)
    stage_b(0, 1)
    stage_a(1, 0)
    stage_x(1, 0)
    stage_own(0)
    stage_d(0, 0)

    plan = [(0, 0, b) for b in (0, 1, 2, 3)]
    plan += [(0, 1, b) for b in (2, 3, 0, 1)]
    plan += [(1, 0, b) for b in (0, 1, 2, 3)]
    plan += [(1, 1, b) for b in (2, 3, 0, 1)]
    plan += [(2, 0, 2), (2, 0, 3), (2, 0, 0), (2, 1, 2)]
    plan += [(2, 1, 3), (2, 0, 1), (2, 1, 0), (2, 1, 1)]

    def head_q(h):
        yq(h).wait_recv()

    before_step = {
        0: [(send_kv, 2, (0, 1))],
        1: [(head_q, 0), (send_q, 2)],
        2: [(stage_a, 1, 1), (stage_x, 1, 1), (stage_c, 0, 1)],
        3: [(stage_b, 1, 0), (stage_d, 0, 1)],
        4: [(share_q, 1)],
        5: [(stage_a, 2, 0), (stage_x, 2, 0)],
        6: [(stage_b, 1, 1)],
        7: [(stage_c, 1, 0), (stage_own, 1), (stage_d, 1, 0)],
        8: [(stage_a, 2, 1), (stage_x, 2, 1)],
        9: [(stage_b, 2, 0), (head_q, 1)],
        10: [(share_q, 2), (combine, 0, 0)],
        11: [(stage_c, 1, 1), (stage_d, 1, 1)],
        12: [(stage_b, 2, 1)],
        13: [(combine, 0, 1)],
        15: [(stage_c, 2, 0), (stage_own, 2), (stage_d, 2, 0), (head_q, 2)],
        17: [(stage_c, 2, 1), (combine, 1, 0)],
        18: [(stage_d, 2, 1)],
        19: [(combine, 1, 1)],
        23: [(combine, 2, 0)],
    }
    bufs = (s_a, s_b)
    fill(*plan[0], s_a)
    for t, (h, unit, b) in enumerate(plan):
        for act, *args in before_step.get(t, ()):
            act(*args)
        after = plan[t + 1] if t + 1 < len(plan) else None
        step(h, unit, b, bufs[t % 2], bufs[(t + 1) % 2], after)
    combine(2, 1)

    landed(txt_land, ht_r)
    r8 = lax.broadcasted_iota(jnp.int32, (8, tr), 0)
    c8 = lax.broadcasted_iota(jnp.int32, (8, tr), 1)
    mine = jnp.where(c8 == r8 + z * trows, 1.0, 0.0).astype(BF)
    out_txt[...] = dot(mine, txt_land[...], ((1,), (0,)))[:trows].astype(BF)

    landed(out_img, hi_r)
    landed(kv_send.at[pl.ds(0, len(others))], zkv_s)
    landed(q_send.at[pl.ds(0, len(others))], zq_s)
    landed(tx_send.at[pl.ds(0, len(others))], zt_s)
    landed(kv_all.at[:, :, :, pl.ds(0, 2 * blk_rows), :], xs_s)
    landed(kv_all.at[:, :, :, pl.ds(0, blk_rows), :], xf_s)
    landed(kv_all.at[:, :, :, pl.ds(0, side), :], sb_s)
    landed(q_all.at[:, pl.ds(0, 2)], yq_s)
    landed(o_send, yo_s)
    landed(l_send, yl_s)
    landed(q_send.at[pl.ds(0, len(others))], hi_s)
    landed(result.at[0, 0, pl.ds(0, LH * len(others) * tr), :], ht_s)


def local(img_qkv, txt_qkv, q_gain, k_gain):
    rows, trows = img_qkv.shape[0], txt_qkv.shape[0]
    width = HEADS * HD
    blk_rows = ZS * (rows + trows)
    n_keys = 8 * blk_rows
    pad = -(-3 * LH * trows // 16) * 16
    dma = pltpu.SemaphoreType.DMA
    vm = pltpu.VMEM
    return pl.pallas_call(
        kernel,
        out_shape=(
            jax.ShapeDtypeStruct((rows, width), BF),
            jax.ShapeDtypeStruct((trows, width), BF),
        ),
        in_specs=[pl.BlockSpec(memory_space=pl.ANY)]
        + [pl.BlockSpec(memory_space=pltpu.VMEM)] * 3,
        out_specs=(pl.BlockSpec(memory_space=pl.ANY), pl.BlockSpec(memory_space=pltpu.VMEM)),
        scratch_shapes=[
            vm((rows, 3 * width), BF),
            vm((GROUPS, LH, 2, rows, HD), BF),
            vm((GROUPS, LH, rows, HD), BF),
            vm((GROUPS, pad, HD), F32),
            vm((GROUPS, pad, HD), BF),
            vm((2, ZS, pad, HD), BF),
            vm((LH, 2, 2, n_keys, HD), BF),
            vm((LH, 4, blk_rows, HD), BF),
            vm((blk_rows, n_keys), F32),
            vm((blk_rows, n_keys), F32),
            vm((4, blk_rows, 2 * HD), F32),
            vm((4, blk_rows, HD), F32),
            vm((LH, 2, blk_rows, HD), BF),
            vm((LH, 2, 8, HD), F32),
            vm((LH, 2, blk_rows, HD), BF),
            vm((LH, 2, 8, HD), F32),
            vm((LH, 2, blk_rows, HD), BF),
            vm((LH, 2, blk_rows, HD), F32),
            vm((LH, 2, blk_rows, HD), BF),
            vm((ZS * trows, width), BF),
            vm((2, rows, HD), F32),
            vm((blk_rows, HD), F32),
            dma((3,)), dma((LH, 2)), dma((LH,)), dma, dma((LH, 2, 2)), dma((LH, 2)),
            dma((LH,)), dma((LH, 2)), dma((LH,)), dma((LH, 2)), dma((LH, 2)), dma, dma, dma((11,)),
        ],
        compiler_params=pltpu.CompilerParams(
            collective_id=0, has_side_effects=True, vmem_limit_bytes=56 * 2**20
        ),
        cost_estimate=pl.CostEstimate(
            flops=4 * LH * 8 * blk_rows * n_keys * HD,
            bytes_accessed=4 * rows * 3 * width,
            transcendentals=LH * 8 * blk_rows * n_keys,
        ),
    )(img_qkv, txt_qkv, q_gain.reshape(1, HD), k_gain.reshape(1, HD))


def solution(mesh):
    in_specs = (P(("blk", "head"), None), P(("blk", "head"), None), P(), P())
    out_specs = (P(("blk", "head"), None), P(("blk", "head"), None))
    return jax.shard_map(local, mesh=mesh, in_specs=in_specs, out_specs=out_specs, check_vma=False)
```
